128 devices in a mesh: row: 16 (over y_hi, z, core), col: 8 (over y_lo, x).
Axes of the slice: x: 4, y: 4 (y_hi: 2, y_lo: 2; y = y_hi * 2 + y_lo), z: 4, core: 2. Of those that a mesh axis runs over, the one named last changes fastest.
Arguments:
- pair_rep: bfloat16 [512, 512, 128], P('row', 'col'), may hold values from -6 to 6
- in_gain: float32 [128], replicated, may hold values from 0.25 to 1.75
- in_bias: float32 [128], replicated, may hold values from -3 to 3
- w_left_gate: bfloat16 [128, 128], replicated, may hold values from -0.5 to 0.5
- w_left: bfloat16 [128, 128], replicated, may hold values from -0.5 to 0.5
- w_right_gate: bfloat16 [128, 128], replicated, may hold values from -0.5 to 0.5
- w_right: bfloat16 [128, 128], replicated, may hold values from -0.5 to 0.5
- out_gain: float32 [128], replicated, may hold values from 0.25 to 1.75
- out_bias: float32 [128], replicated, may hold values from -3 to 3
- w_out_gate: bfloat16 [128, 128], replicated, may hold values from -0.5 to 0.5
- w_out: bfloat16 [128, 128], replicated, may hold values from -0.5 to 0.5
Outputs:
- update: float32 [512, 512, 128], P('row', 'col')
The draws below stay inside these ranges and needn't reach their ends.
All inputs are finite; a program needn't handle non-finite values.
Results may differ from the reference program's by a relative error of at most 0.0037.
Values may be sent and summed in bfloat16 or wider, within the bound.
No kernel may reach another device: no remote copies, remote signals or barrier semaphores. Data moves between devices by JAX's collectives and lax.ppermute only.
A program may use at most 128 MiB of HBM per device.

```python
import jax
import jax.numpy as jnp
from jax import lax

CZ = 128
CH = 128
N_RES = 512


def shard_levels(rng, dims, shards, smallest, largest):
    def one(dim, parts):
        draws = jax.random.uniform(jax.random.fold_in(jax.random.fold_in(rng, 6), dim), (parts,), jnp.float32, smallest / len(shards), largest / len(shards))
        return jnp.repeat(jnp.exp(draws), dims[dim] // parts).reshape((-1,) + (1,) * (len(dims) - dim - 1))

    loudness = one(*shards[0])
    for cut in shards[1:]:
        loudness = loudness * one(*cut)
    return loudness


def centred(own_key, shape, deviation, limit, split=(), kind=jnp.bfloat16):
    drawn = deviation * jax.random.normal(own_key, shape, jnp.float32)
    if split:
        drawn = drawn * shard_levels(own_key, shape, split, -0.22, 0.18)
    return jnp.clip(drawn, -limit, limit).astype(kind)


def setup_inputs(seed: int = 0) -> dict:
    key_list = jax.random.split(jax.random.key(seed), 12)
    return {
        "pair_rep": centred(key_list[0], (N_RES, N_RES, CZ), 1.0, 6.0, ((0, 16), (1, 8))),
        "in_gain": jnp.clip(1.0 + 0.15 * jax.random.normal(key_list[1], (CZ,), jnp.float32), 0.25, 1.75),
        "in_bias": centred(key_list[2], (CZ,), 0.5, 3.0, (), jnp.float32),
        "w_left_gate": centred(key_list[3], (CZ, CH), CZ ** -0.5, 0.5),
        "w_left": centred(key_list[4], (CZ, CH), CZ ** -0.5, 0.5),
        "w_right_gate": centred(key_list[5], (CZ, CH), CZ ** -0.5, 0.5),
        "w_right": centred(key_list[6], (CZ, CH), CZ ** -0.5, 0.5),
        "out_gain": jnp.clip(1.0 + 0.15 * jax.random.normal(key_list[7], (CH,), jnp.float32), 0.25, 1.75),
        "out_bias": centred(key_list[8], (CH,), 0.5, 3.0, (), jnp.float32),
        "w_out_gate": centred(key_list[9], (CZ, CZ), CZ ** -0.5, 0.5),
        "w_out": centred(key_list[10], (CH, CZ), CH ** -0.5, 0.5),
    }


EPS = 1e-05

def layer_norm(values, norm_gain, norm_bias):
    mean_val = lax.optimization_barrier(jnp.mean(values, -1, keepdims=True))
    variance = lax.optimization_barrier(jnp.mean(jnp.square(values - mean_val), -1, keepdims=True))
    return (values - mean_val) * lax.rsqrt(variance + EPS) * norm_gain + norm_bias

def gated_proj(flat_rows, w_gate, w_proj):
    gate_val = jnp.dot(flat_rows, w_gate, preferred_element_type=jnp.float32)
    proj_val = jnp.dot(flat_rows, w_proj, preferred_element_type=jnp.float32)
    return (jax.nn.sigmoid(gate_val) * proj_val).astype(jnp.bfloat16)

def reference(pair_rep, in_gain, in_bias, w_left_gate, w_left, w_right_gate, w_right, out_gain, out_bias, w_out_gate, w_out):
    normed = layer_norm(pair_rep.astype(jnp.float32), in_gain, in_bias).astype(jnp.bfloat16)
    flat_rows = normed.reshape(N_RES * N_RES, CZ)
    left_proj = gated_proj(flat_rows, w_left_gate, w_left).reshape(N_RES, N_RES, CH)
    right_proj = gated_proj(flat_rows, w_right_gate, w_right).reshape(N_RES, N_RES, CH)
    left_chan = jnp.transpose(left_proj, (2, 0, 1)).astype(jnp.float32)
    right_chan = jnp.transpose(right_proj, (2, 0, 1)).astype(jnp.float32)
    mixed_sum = jnp.einsum('cik,cjk->ijc', left_chan, right_chan)
    mixed_norm = layer_norm(mixed_sum, out_gain, out_bias).astype(jnp.bfloat16)
    gate_act = jax.nn.sigmoid(jnp.dot(flat_rows, w_out_gate, preferred_element_type=jnp.float32))
    projected = jnp.dot(mixed_norm.reshape(N_RES * N_RES, CH), w_out, preferred_element_type=jnp.float32)
    return (gate_act * projected).reshape(N_RES, N_RES, CZ)
```

```python
import jax
import jax.numpy as jnp
from jax import lax
from jax.experimental import pallas as pl
from jax.experimental.pallas import tpu as pltpu
from jax.sharding import PartitionSpec as P

EPS = 1e-05
CH = 128
ROWS, COLS = 32, 64
SLABS = ROWS * COLS // 128
HALF = ROWS // 2
POSITIONS = ROWS * COLS


def pair_positions(slab):
    return slab * COLS, HALF * COLS + slab * COLS


def input_norm(x_ref, gain, bias, slab):
    low, high = pair_positions(slab)
    values = jnp.concatenate([x_ref[pl.ds(low, COLS), :], x_ref[pl.ds(high, COLS), :]], 0)
    values = values.astype(jnp.float32)
    centred = values - jnp.mean(values, -1, keepdims=True)
    variance = jnp.mean(jnp.square(centred), -1, keepdims=True)
    return (centred * lax.rsqrt(variance + EPS) * gain + bias).astype(jnp.bfloat16)


def project_kernel(x_ref, gain_ref, bias_ref, wlg_ref, wl_ref, wrg_ref, wr_ref, out_ref, wide):
    weights = jnp.concatenate(
        [jnp.transpose(w_ref[...]) for w_ref in (wlg_ref, wl_ref, wrg_ref, wr_ref)], 0
    )
    gain, bias = gain_ref[...], bias_ref[...]
    for pair in range(SLABS // 2):
        normed = jnp.concatenate(
            [input_norm(x_ref, gain, bias, 2 * pair + member) for member in range(2)], 0
        )
        both = lax.dot_general(
            weights, normed, (((1,), (1,)), ((), ())), preferred_element_type=jnp.float32
        )
        left = jax.nn.sigmoid(both[:CH]) * both[CH : 2 * CH]
        right = jax.nn.sigmoid(both[2 * CH : 3 * CH]) * both[3 * CH :]
        for member in range(2):
            slab = 2 * pair + member
            lanes = slice(member * 128, member * 128 + 128)
            wide[pl.ds(slab, CH, stride=2 * SLABS), :] = left[:, lanes]
            wide[pl.ds(SLABS + slab, CH, stride=2 * SLABS), :] = right[:, lanes]
    out_ref[...] = wide[...].astype(jnp.bfloat16)


def gate_kernel(x_ref, gain_ref, bias_ref, w_ref, out_ref):
    gain, bias, weights = gain_ref[...], bias_ref[...], w_ref[...]
    for slab in range(SLABS):
        normed = input_norm(x_ref, gain, bias, slab)
        gate = jax.nn.sigmoid(jnp.dot(normed, weights, preferred_element_type=jnp.float32))
        low, high = pair_positions(slab)
        out_ref[pl.ds(low, COLS), :] = gate[:COLS]
        out_ref[pl.ds(high, COLS), :] = gate[COLS:]


def side_by_side(first, second, half):
    lanes = slice(half * 64, half * 64 + 64)
    return jnp.concatenate([first[:, lanes], second[:, lanes]], 1)


def mix_kernel(n_row, n_col, in_ref, out_ref, left, right):
    for r in range(n_row):
        for m in range(n_col // 2):
            start = (r * n_col + 2 * m) * 2 * SLABS
            first = in_ref[pl.ds(start, 2 * SLABS), :]
            second = in_ref[pl.ds(start + 2 * SLABS, 2 * SLABS), :]
            lanes = slice(m * 128, m * 128 + 128)
            for half in range(2):
                tile = side_by_side(first, second, half)
                rows = pl.ds(r * ROWS + half * HALF, HALF)
                left[rows, lanes] = tile[:SLABS]
                right[rows, lanes] = tile[SLABS:]
    for r in range(0, n_row, 4):
        block = lax.dot_general(
            left[pl.ds(r * ROWS, 4 * ROWS), :],
            right[...],
            (((1,), (1,)), ((), ())),
            preferred_element_type=jnp.float32,
        )
        for inner in range(4):
            for m in range(n_col // 2):
                lanes = slice(m * 128, m * 128 + 128)
                top = block[inner * ROWS : inner * ROWS + HALF, lanes]
                bottom = block[inner * ROWS + HALF : (inner + 1) * ROWS, lanes]
                for half in range(2):
                    start = ((r + inner) * n_col + 2 * m + half) * SLABS
                    out_ref[pl.ds(start, SLABS), :] = side_by_side(top, bottom, half).astype(
                        jnp.bfloat16
                    )


def finish_kernel(mixed_ref, gate_ref, gain_ref, bias_ref, w_ref, out_ref, wide):
    wide[...] = mixed_ref[...].astype(jnp.float32)
    total = jnp.zeros((SLABS, 128), jnp.float32)
    for c in range(CH):
        total += wide[pl.ds(c * SLABS, SLABS), :]
    mean = total / CH
    square = jnp.zeros((SLABS, 128), jnp.float32)
    for c in range(CH):
        square += jnp.square(wide[pl.ds(c * SLABS, SLABS), :] - mean)
    scale = lax.rsqrt(square / CH + EPS)
    gain = jnp.broadcast_to(gain_ref[...], (CH, 128))
    bias = jnp.broadcast_to(bias_ref[...], (CH, 128))
    weights = w_ref[...]
    for slab in range(SLABS):
        values = wide[pl.ds(slab, CH, stride=SLABS), :]
        normed = (values - mean[slab : slab + 1]) * scale[slab : slab + 1] * gain + bias
        projected = lax.dot_general(
            normed.astype(jnp.bfloat16),
            weights,
            (((0,), (0,)), ((), ())),
            preferred_element_type=jnp.float32,
        )
        low, high = pair_positions(slab)
        out_ref[pl.ds(low, COLS), :] = gate_ref[pl.ds(low, COLS), :] * projected[:COLS]
        out_ref[pl.ds(high, COLS), :] = gate_ref[pl.ds(high, COLS), :] * projected[COLS:]


def per_device(
    pair_rep,
    in_gain,
    in_bias,
    w_left_gate,
    w_left,
    w_right_gate,
    w_right,
    out_gain,
    out_bias,
    w_out_gate,
    w_out,
):
    n_row, n_col = lax.axis_size("row"), lax.axis_size("col")
    devices = n_row * n_col
    params = pltpu.CompilerParams(vmem_limit_bytes=48 << 20)
    flat = pair_rep.reshape(POSITIONS, CH)
    in_gain, in_bias = in_gain.reshape(1, CH), in_bias.reshape(1, CH)
    sent = pl.pallas_call(
        project_kernel,
        out_shape=jax.ShapeDtypeStruct((CH * 2 * SLABS, 128), jnp.bfloat16),
        scratch_shapes=[pltpu.VMEM((CH * 2 * SLABS, 128), jnp.float32)],
        compiler_params=params,
        name="project",
    )(flat, in_gain, in_bias, w_left_gate, w_left, w_right_gate, w_right)
    arrived = lax.all_to_all(
        sent.reshape(devices, 2 * SLABS, 128), ("row", "col"), 0, 0, tiled=True
    )
    gate_act = pl.pallas_call(
        gate_kernel,
        out_shape=jax.ShapeDtypeStruct((POSITIONS, CH), jnp.float32),
        compiler_params=params,
        cost_estimate=pl.CostEstimate(
            flops=2 * POSITIONS * CH * CH, bytes_accessed=3 << 19, transcendentals=POSITIONS * CH
        ),
        name="gate",
    )(flat, in_gain, in_bias, w_out_gate)
    n_res = n_row * ROWS
    mixed = pl.pallas_call(
        lambda *refs: mix_kernel(n_row, n_col, *refs),
        out_shape=jax.ShapeDtypeStruct((devices * SLABS, 128), jnp.bfloat16),
        scratch_shapes=[pltpu.VMEM((n_res, n_res), jnp.bfloat16)] * 2,
        compiler_params=params,
        name="mix",
    )(arrived.reshape(devices * 2 * SLABS, 128))
    returned = lax.all_to_all(
        mixed.reshape(devices, SLABS, 128), ("row", "col"), 0, 0, tiled=True
    )
    update = pl.pallas_call(
        finish_kernel,
        out_shape=jax.ShapeDtypeStruct((POSITIONS, CH), jnp.float32),
        scratch_shapes=[pltpu.VMEM((CH * SLABS, 128), jnp.float32)],
        compiler_params=params,
        name="finish",
    )(
        returned.reshape(CH * SLABS, 128),
        gate_act,
        out_gain.reshape(CH, 1),
        out_bias.reshape(CH, 1),
        w_out,
    )
    return update.reshape(ROWS, COLS, CH)


def solution(mesh):
    placed = (P("row", "col", None), P(), P(), P(), P(), P(), P(), P(), P(), P(), P())
    return jax.shard_map(
        per_device, mesh=mesh, in_specs=placed, out_specs=P("row", "col", None), check_vma=False
    )
```

```python
import jax
import jax.numpy as jnp
from jax import lax
from jax.experimental import pallas as pl
from jax.experimental.pallas import tpu as pltpu
from jax.sharding import PartitionSpec as P

EPS = 1e-05
CH = 128
ROWS, COLS = 32, 64
SLABS = ROWS * COLS // 128
HALF = ROWS // 2
POSITIONS = ROWS * COLS
PITCH = 36
OUT_PITCH = 20
PIECES = 2
PIECE_ROWS = POSITIONS // 2 // PIECES


def in_hbm(array):
    return pltpu.with_memory_space_constraint(array, pltpu.HBM)


def pair_positions(slab):
    return slab * COLS, HALF * COLS + slab * COLS


def input_norm(x_ref, gain, bias, slab):
    low, high = pair_positions(slab)
    values = jnp.concatenate([x_ref[pl.ds(low, COLS), :], x_ref[pl.ds(high, COLS), :]], 0)
    values = values.astype(jnp.float32)
    centred = values - jnp.mean(values, -1, keepdims=True)
    variance = jnp.mean(jnp.square(centred), -1, keepdims=True)
    return (centred * lax.rsqrt(variance + EPS) * gain + bias).astype(jnp.bfloat16)


def project_kernel(
    x_hbm, gain_hbm, bias_hbm, wlg_hbm, wl_hbm, wrg_hbm, wr_hbm, out_ref, x, norm, kept, wide, sems
):
    copies = [
        pltpu.make_async_copy(gain_hbm, norm.at[pl.ds(0, 1)], sems.at[0]),
        pltpu.make_async_copy(bias_hbm, norm.at[pl.ds(1, 1)], sems.at[1]),
    ]
    for k, w_hbm in enumerate((wlg_hbm, wl_hbm, wrg_hbm, wr_hbm)):
        copies.append(pltpu.make_async_copy(w_hbm, kept.at[k], sems.at[2 + k]))
    pieces = [[pltpu.make_async_copy(x_hbm, x, sems.at[6])]]
    for copy in pieces[0] + copies + sum(pieces[1:], []):
        copy.start()
    for copy in pieces[0] + copies:
        copy.wait()
    weights = jnp.concatenate([jnp.transpose(kept[k]) for k in range(4)], 0)
    gain, bias = norm[0:1, :], norm[1:2, :]
    for pair in range(SLABS // 2):
        normed = jnp.concatenate(
            [input_norm(x, gain, bias, 2 * pair + member) for member in range(2)], 0
        )
        both = lax.dot_general(
            weights, normed, (((1,), (1,)), ((), ())), preferred_element_type=jnp.float32
        )
        left = jax.nn.sigmoid(both[:CH]) * both[CH : 2 * CH]
        right = jax.nn.sigmoid(both[2 * CH : 3 * CH]) * both[3 * CH :]
        for member in range(2):
            slab = 2 * pair + member
            lanes = slice(member * 128, member * 128 + 128)
            wide[pl.ds(slab, CH, stride=PITCH), :] = left[:, lanes]
            wide[pl.ds(SLABS + slab, CH, stride=PITCH), :] = right[:, lanes]
    for c in range(CH):
        out_ref[pl.ds(c * 2 * SLABS, 2 * SLABS), :] = wide[pl.ds(c * PITCH, 2 * SLABS), :].astype(jnp.bfloat16)


def gate_kernel(x_ref, gain_ref, bias_ref, w_ref, out_ref):
    gain, bias, weights = gain_ref[...], bias_ref[...], w_ref[...]
    for slab in range(SLABS):
        normed = input_norm(x_ref, gain, bias, slab)
        gate = jax.nn.sigmoid(jnp.dot(normed, weights, preferred_element_type=jnp.float32))
        low, high = pair_positions(slab)
        out_ref[pl.ds(low, COLS), :] = gate[:COLS]
        out_ref[pl.ds(high, COLS), :] = gate[COLS:]


def side_by_side(first, second, half):
    lanes = slice(half * 64, half * 64 + 64)
    return jnp.concatenate([first[:, lanes], second[:, lanes]], 1)


def mix_kernel(n_row, n_col, in_ref, out_hbm, left, right, out_ref, sems):
    copies = []
    for r in range(n_row):
        for m in range(n_col // 2):
            start = (r * n_col + 2 * m) * 2 * SLABS
            first = in_ref[pl.ds(start, 2 * SLABS), :]
            second = in_ref[pl.ds(start + 2 * SLABS, 2 * SLABS), :]
            lanes = slice(m * 128, m * 128 + 128)
            for half in range(2):
                tile = side_by_side(first, second, half)
                rows = pl.ds(r * ROWS + half * HALF, HALF)
                left[rows, lanes] = tile[:SLABS]
                right[rows, lanes] = tile[SLABS:]
    for r in range(0, n_row, 4):
        block = lax.dot_general(
            left[pl.ds(r * ROWS, 4 * ROWS), :],
            right[...],
            (((1,), (1,)), ((), ())),
            preferred_element_type=jnp.float32,
        )
        for inner in range(4):
            for m in range(n_col // 2):
                lanes = slice(m * 128, m * 128 + 128)
                top = block[inner * ROWS : inner * ROWS + HALF, lanes]
                bottom = block[inner * ROWS + HALF : (inner + 1) * ROWS, lanes]
                for half in range(2):
                    start = ((r + inner) * n_col + 2 * m + half) * SLABS
                    out_ref[pl.ds(start, SLABS), :] = side_by_side(top, bottom, half).astype(
                        jnp.bfloat16
                    )
        rows = pl.ds(r * n_col * SLABS, 4 * n_col * SLABS)
        copies.append(pltpu.make_async_copy(out_ref.at[rows], out_hbm.at[rows], sems.at[r // 4]))
        copies[-1].start()
    for copy in copies:
        copy.wait()


def finish_kernel(
    mixed_ref, gate_ref, gain_ref, bias_ref, w_ref, out_hbm, wide, out_ref, sems
):
    copies = []
    for c in range(CH):
        wide[pl.ds(c * OUT_PITCH, SLABS), :] = mixed_ref[pl.ds(c * SLABS, SLABS), :].astype(jnp.float32)
    total = jnp.zeros((SLABS, 128), jnp.float32)
    for c in range(CH):
        total += wide[pl.ds(c * OUT_PITCH, SLABS), :]
    mean = total / CH
    square = jnp.zeros((SLABS, 128), jnp.float32)
    for c in range(CH):
        square += jnp.square(wide[pl.ds(c * OUT_PITCH, SLABS), :] - mean)
    scale = lax.rsqrt(square / CH + EPS)
    gain = jnp.broadcast_to(gain_ref[...], (CH, 128))
    bias = jnp.broadcast_to(bias_ref[...], (CH, 128))
    weights = w_ref[...]
    for slab in range(SLABS):
        values = wide[pl.ds(slab, CH, stride=OUT_PITCH), :]
        normed = (values - mean[slab : slab + 1]) * scale[slab : slab + 1] * gain + bias
        projected = lax.dot_general(
            normed.astype(jnp.bfloat16),
            weights,
            (((0,), (0,)), ((), ())),
            preferred_element_type=jnp.float32,
        )
        low, high = pair_positions(slab)
        out_ref[pl.ds(low, COLS), :] = gate_ref[pl.ds(low, COLS), :] * projected[:COLS]
        out_ref[pl.ds(high, COLS), :] = gate_ref[pl.ds(high, COLS), :] * projected[COLS:]
        if (slab + 1) % (SLABS // PIECES) == 0:
            for half in range(2):
                rows = pl.ds((half * PIECES + slab // (SLABS // PIECES)) * PIECE_ROWS, PIECE_ROWS)
                copies.append(
                    pltpu.make_async_copy(
                        out_ref.at[rows], out_hbm.at[rows], sems.at[len(copies)]
                    )
                )
                copies[-1].start()
    for copy in copies:
        copy.wait()


def per_device(
    pair_rep,
    in_gain,
    in_bias,
    w_left_gate,
    w_left,
    w_right_gate,
    w_right,
    out_gain,
    out_bias,
    w_out_gate,
    w_out,
):
    n_row, n_col = lax.axis_size("row"), lax.axis_size("col")
    devices = n_row * n_col
    params = pltpu.CompilerParams(vmem_limit_bytes=48 << 20)
    flat = pair_rep.reshape(POSITIONS, CH)
    in_gain, in_bias = in_gain.reshape(1, CH), in_bias.reshape(1, CH)
    sent = pl.pallas_call(
        project_kernel,
        out_shape=jax.ShapeDtypeStruct((CH * 2 * SLABS, 128), jnp.bfloat16),
        in_specs=[pl.BlockSpec(memory_space=pltpu.HBM)] * 7,
        scratch_shapes=[
            pltpu.VMEM((POSITIONS, CH), jnp.bfloat16),
            pltpu.VMEM((2, CH), jnp.float32),
            pltpu.VMEM((4, CH, CH), jnp.bfloat16),
            pltpu.VMEM((CH * PITCH, 128), jnp.float32),
            pltpu.SemaphoreType.DMA((6 + 2 * PIECES,)),
        ],
        compiler_params=params,
        name="project",
    )(*map(in_hbm, (flat, in_gain, in_bias, w_left_gate, w_left, w_right_gate, w_right)))
    arrived = lax.all_to_all(
        sent.reshape(devices, 2 * SLABS, 128), ("row", "col"), 0, 0, tiled=True
    )
    gate_act = pl.pallas_call(
        gate_kernel,
        out_shape=jax.ShapeDtypeStruct((POSITIONS, CH), jnp.float32),
        compiler_params=params,
        cost_estimate=pl.CostEstimate(
            flops=2 * POSITIONS * CH * CH, bytes_accessed=3 << 19, transcendentals=POSITIONS * CH
        ),
        name="gate",
    )(flat, in_gain, in_bias, w_out_gate)
    n_res = n_row * ROWS
    mixed = pl.pallas_call(
        lambda *refs: mix_kernel(n_row, n_col, *refs),
        out_shape=jax.ShapeDtypeStruct((devices * SLABS, 128), jnp.bfloat16),
        out_specs=pl.BlockSpec(memory_space=pltpu.HBM),
        scratch_shapes=[
            pltpu.VMEM((n_res, n_res), jnp.bfloat16),
            pltpu.VMEM((n_res, n_res), jnp.bfloat16),
            pltpu.VMEM((devices * SLABS, 128), jnp.bfloat16),
            pltpu.SemaphoreType.DMA((n_row // 4,)),
        ],
        compiler_params=params,
        name="mix",
    )(arrived.reshape(devices * 2 * SLABS, 128))
    returned = lax.all_to_all(
        mixed.reshape(devices, SLABS, 128), ("row", "col"), 0, 0, tiled=True
    )
    update = pl.pallas_call(
        finish_kernel,
        out_shape=jax.ShapeDtypeStruct((POSITIONS, CH), jnp.float32),
        out_specs=pl.BlockSpec(memory_space=pltpu.HBM),
        scratch_shapes=[
            pltpu.VMEM((CH * OUT_PITCH, 128), jnp.float32),
            pltpu.VMEM((POSITIONS, CH), jnp.float32),
            pltpu.SemaphoreType.DMA((2 * PIECES,)),
        ],
        compiler_params=params,
        name="finish",
    )(
        returned.reshape(CH * SLABS, 128),
        gate_act,
        out_gain.reshape(CH, 1),
        out_bias.reshape(CH, 1),
        w_out,
    )
    return update.reshape(ROWS, COLS, CH)


def solution(mesh):
    placed = (P("row", "col", None), P(), P(), P(), P(), P(), P(), P(), P(), P(), P())
    return jax.shard_map(
        per_device, mesh=mesh, in_specs=placed, out_specs=P("row", "col", None), check_vma=False
    )
```

```python
import jax
import jax.numpy as jnp
from jax import lax
from jax.experimental import pallas as pl
from jax.experimental.pallas import tpu as pltpu
from jax.sharding import PartitionSpec as P

EPS = 1e-05
CH = 128
ROWS, COLS = 32, 64
SLABS = ROWS * COLS // 128
HALF = ROWS // 2
POSITIONS = ROWS * COLS
PITCH = 36
OUT_PITCH = 20


def in_hbm(array):
    return pltpu.with_memory_space_constraint(array, pltpu.HBM)


def pair_positions(slab):
    return slab * COLS, HALF * COLS + slab * COLS


def input_norm(x_ref, gain, bias, slab):
    low, high = pair_positions(slab)
    values = jnp.concatenate([x_ref[pl.ds(low, COLS), :], x_ref[pl.ds(high, COLS), :]], 0)
    values = values.astype(jnp.float32)
    centred = values - jnp.mean(values, -1, keepdims=True)
    variance = jnp.mean(jnp.square(centred), -1, keepdims=True)
    return (centred * lax.rsqrt(variance + EPS) * gain + bias).astype(jnp.bfloat16)


def project_kernel(
    x_hbm, gain_hbm, bias_hbm, wlg_hbm, wl_hbm, wrg_hbm, wr_hbm, out_ref, normed_ref, x, norm, kept, wide, sems
):
    copies = [
        pltpu.make_async_copy(gain_hbm, norm.at[pl.ds(0, 1)], sems.at[0]),
        pltpu.make_async_copy(bias_hbm, norm.at[pl.ds(1, 1)], sems.at[1]),
    ]
    for k, w_hbm in enumerate((wlg_hbm, wl_hbm, wrg_hbm, wr_hbm)):
        copies.append(pltpu.make_async_copy(w_hbm, kept.at[k], sems.at[2 + k]))
    pieces = [[pltpu.make_async_copy(x_hbm, x, sems.at[6])]]
    for copy in pieces[0] + copies + sum(pieces[1:], []):
        copy.start()
    for copy in pieces[0] + copies:
        copy.wait()
    weights = jnp.concatenate([jnp.transpose(kept[k]) for k in range(4)], 0)
    gain, bias = norm[0:1, :], norm[1:2, :]
    for pair in range(SLABS // 2):
        normed = jnp.concatenate(
            [input_norm(x, gain, bias, 2 * pair + member) for member in range(2)], 0
        )
        normed_ref[pl.ds(pair * 256, 256), :] = normed
        both = lax.dot_general(
            weights, normed, (((1,), (1,)), ((), ())), preferred_element_type=jnp.float32
        )
        left = jax.nn.sigmoid(both[:CH]) * both[CH : 2 * CH]
        right = jax.nn.sigmoid(both[2 * CH : 3 * CH]) * both[3 * CH :]
        for member in range(2):
            slab = 2 * pair + member
            lanes = slice(member * 128, member * 128 + 128)
            wide[pl.ds(slab, CH, stride=PITCH), :] = left[:, lanes]
            wide[pl.ds(SLABS + slab, CH, stride=PITCH), :] = right[:, lanes]
    for c in range(CH):
        out_ref[pl.ds(c * 2 * SLABS, 2 * SLABS), :] = wide[pl.ds(c * PITCH, 2 * SLABS), :].astype(jnp.bfloat16)


def side_by_side(first, second, half):
    lanes = slice(half * 64, half * 64 + 64)
    return jnp.concatenate([first[:, lanes], second[:, lanes]], 1)


def mix_kernel(
    n_row, n_col, in_ref, gain_hbm, bias_hbm, out_ref, gain_ref, bias_ref, left, right, sems
):
    copies = [
        pltpu.make_async_copy(gain_hbm, gain_ref, sems.at[0]),
        pltpu.make_async_copy(bias_hbm, bias_ref, sems.at[1]),
    ]
    for copy in copies:
        copy.start()
    for r in range(n_row):
        for m in range(n_col // 2):
            start = (r * n_col + 2 * m) * 2 * SLABS
            first = in_ref[pl.ds(start, 2 * SLABS), :]
            second = in_ref[pl.ds(start + 2 * SLABS, 2 * SLABS), :]
            lanes = slice(m * 128, m * 128 + 128)
            for half in range(2):
                tile = side_by_side(first, second, half)
                rows = pl.ds(r * ROWS + half * HALF, HALF)
                left[rows, lanes] = tile[:SLABS]
                right[rows, lanes] = tile[SLABS:]
    for r in range(0, n_row, 4):
        block = lax.dot_general(
            left[pl.ds(r * ROWS, 4 * ROWS), :],
            right[...],
            (((1,), (1,)), ((), ())),
            preferred_element_type=jnp.float32,
        )
        for inner in range(4):
            for m in range(n_col // 2):
                lanes = slice(m * 128, m * 128 + 128)
                top = block[inner * ROWS : inner * ROWS + HALF, lanes]
                bottom = block[inner * ROWS + HALF : (inner + 1) * ROWS, lanes]
                for half in range(2):
                    start = ((r + inner) * n_col + 2 * m + half) * SLABS
                    out_ref[pl.ds(start, SLABS), :] = side_by_side(top, bottom, half).astype(
                        jnp.bfloat16
                    )
    for copy in copies:
        copy.wait()


def finish_kernel(mixed_ref, normed_ref, gain_ref, bias_ref, wg_ref, w_ref, out_hbm, wide, out_ref, sem):
    for c in range(CH):
        wide[pl.ds(c * OUT_PITCH, SLABS), :] = mixed_ref[pl.ds(c * SLABS, SLABS), :].astype(
            jnp.float32
        )
    total = jnp.zeros((SLABS, 128), jnp.float32)
    for c in range(CH):
        total += wide[pl.ds(c * OUT_PITCH, SLABS), :]
    mean = total / CH
    square = jnp.zeros((SLABS, 128), jnp.float32)
    for c in range(CH):
        square += jnp.square(wide[pl.ds(c * OUT_PITCH, SLABS), :] - mean)
    scale = lax.rsqrt(square / CH + EPS)
    gain = jnp.transpose(jnp.broadcast_to(gain_ref[...], (128, CH)))
    bias = jnp.transpose(jnp.broadcast_to(bias_ref[...], (128, CH)))
    gate_weights, weights = wg_ref[...], w_ref[...]
    for slab in range(SLABS):
        values = wide[pl.ds(slab, CH, stride=OUT_PITCH), :]
        normed = (values - mean[slab : slab + 1]) * scale[slab : slab + 1] * gain + bias
        projected = lax.dot_general(
            normed.astype(jnp.bfloat16),
            weights,
            (((0,), (0,)), ((), ())),
            preferred_element_type=jnp.float32,
        )
        gate = jnp.dot(
            normed_ref[pl.ds(slab * 128, 128), :], gate_weights, preferred_element_type=jnp.float32
        )
        update = jax.nn.sigmoid(gate) * projected
        low, high = pair_positions(slab)
        out_ref[pl.ds(low, COLS), :] = update[:COLS]
        out_ref[pl.ds(high, COLS), :] = update[COLS:]
    copy = pltpu.make_async_copy(out_ref, out_hbm, sem)
    copy.start()
    copy.wait()


def per_device(
    pair_rep,
    in_gain,
    in_bias,
    w_left_gate,
    w_left,
    w_right_gate,
    w_right,
    out_gain,
    out_bias,
    w_out_gate,
    w_out,
):
    n_row, n_col = lax.axis_size("row"), lax.axis_size("col")
    devices = n_row * n_col
    params = pltpu.CompilerParams(vmem_limit_bytes=48 << 20)
    flat = pair_rep.reshape(POSITIONS, CH)
    in_gain, in_bias = in_gain.reshape(1, CH), in_bias.reshape(1, CH)
    sent, normed = pl.pallas_call(
        project_kernel,
        out_shape=(
            jax.ShapeDtypeStruct((CH * 2 * SLABS, 128), jnp.bfloat16),
            jax.ShapeDtypeStruct((POSITIONS, CH), jnp.bfloat16),
        ),
        in_specs=[pl.BlockSpec(memory_space=pltpu.HBM)] * 7,
        scratch_shapes=[
            pltpu.VMEM((POSITIONS, CH), jnp.bfloat16),
            pltpu.VMEM((2, CH), jnp.float32),
            pltpu.VMEM((4, CH, CH), jnp.bfloat16),
            pltpu.VMEM((CH * PITCH, 128), jnp.float32),
            pltpu.SemaphoreType.DMA((7,)),
        ],
        compiler_params=params,
        name="project",
    )(*map(in_hbm, (flat, in_gain, in_bias, w_left_gate, w_left, w_right_gate, w_right)))
    arrived = lax.all_to_all(
        sent.reshape(devices, 2 * SLABS, 128), ("row", "col"), 0, 0, tiled=True
    )
    n_res = n_row * ROWS
    mixed, out_gain, out_bias = pl.pallas_call(
        lambda *refs: mix_kernel(n_row, n_col, *refs),
        out_shape=(
            jax.ShapeDtypeStruct((devices * SLABS, 128), jnp.bfloat16),
            jax.ShapeDtypeStruct((1, CH), jnp.float32),
            jax.ShapeDtypeStruct((1, CH), jnp.float32),
        ),
        in_specs=[pl.BlockSpec(memory_space=space) for space in (pltpu.VMEM, pltpu.HBM, pltpu.HBM)],
        scratch_shapes=[
            pltpu.VMEM((n_res, n_res), jnp.bfloat16),
            pltpu.VMEM((n_res, n_res), jnp.bfloat16),
            pltpu.SemaphoreType.DMA((2,)),
        ],
        compiler_params=params,
        name="mix",
    )(
        arrived.reshape(devices * 2 * SLABS, 128),
        in_hbm(out_gain.reshape(1, CH)),
        in_hbm(out_bias.reshape(1, CH)),
    )
    returned = lax.all_to_all(
        mixed.reshape(devices, SLABS, 128), ("row", "col"), 0, 0, tiled=True
    )
    update = pl.pallas_call(
        finish_kernel,
        out_shape=jax.ShapeDtypeStruct((POSITIONS, CH), jnp.float32),
        out_specs=pl.BlockSpec(memory_space=pltpu.HBM),
        scratch_shapes=[
            pltpu.VMEM((CH * OUT_PITCH, 128), jnp.float32),
            pltpu.VMEM((POSITIONS, CH), jnp.float32),
            pltpu.SemaphoreType.DMA,
        ],
        compiler_params=params,
        name="finish",
    )(
        returned.reshape(CH * SLABS, 128),
        normed,
        out_gain,
        out_bias,
        w_out_gate,
        w_out,
    )
    return update.reshape(ROWS, COLS, CH)


def solution(mesh):
    placed = (P("row", "col", None), P(), P(), P(), P(), P(), P(), P(), P(), P(), P())
    return jax.shard_map(
        per_device, mesh=mesh, in_specs=placed, out_specs=P("row", "col", None), check_vma=False
    )
```

```python
import jax
import jax.numpy as jnp
from jax import lax
from jax.experimental import pallas as pl
from jax.experimental.pallas import tpu as pltpu
from jax.sharding import PartitionSpec as P

EPS = 1e-05
CH = 128
ROWS, COLS = 32, 64
SLABS = ROWS * COLS // 128
HALF = ROWS // 2
POSITIONS = ROWS * COLS
PITCH = 36
OUT_PITCH = 20


def in_hbm(array):
    return pltpu.with_memory_space_constraint(array, pltpu.HBM)


def pair_positions(slab):
    return slab * COLS, HALF * COLS + slab * COLS


def input_norm(x_ref, gain, bias, slab):
    low, high = pair_positions(slab)
    values = jnp.concatenate([x_ref[pl.ds(low, COLS), :], x_ref[pl.ds(high, COLS), :]], 0)
    values = values.astype(jnp.float32)
    centred = values - jnp.mean(values, -1, keepdims=True)
    variance = jnp.mean(jnp.square(centred), -1, keepdims=True)
    return (centred * lax.rsqrt(variance + EPS) * gain + bias).astype(jnp.bfloat16)


def project_kernel(
    x_hbm, gain_hbm, bias_hbm, wlg_hbm, wl_hbm, wrg_hbm, wr_hbm, out_ref, normed_ref, x, norm, kept, wide, sems
):
    copies = [
        pltpu.make_async_copy(gain_hbm, norm.at[pl.ds(0, 1)], sems.at[0]),
        pltpu.make_async_copy(bias_hbm, norm.at[pl.ds(1, 1)], sems.at[1]),
    ]
    for k, w_hbm in enumerate((wlg_hbm, wl_hbm, wrg_hbm, wr_hbm)):
        copies.append(pltpu.make_async_copy(w_hbm, kept.at[k], sems.at[2 + k]))
    copy_x = pltpu.make_async_copy(x_hbm, x, sems.at[6])
    for copy in [copy_x] + copies:
        copy.start()
    for copy in copies:
        copy.wait()
    weights = jnp.concatenate([jnp.transpose(kept[k]) for k in range(4)], 0)
    gain, bias = norm[0:1, :], norm[1:2, :]
    copy_x.wait()
    for pair in range(SLABS // 2):
        normed = jnp.concatenate(
            [input_norm(x, gain, bias, 2 * pair + member) for member in range(2)], 0
        )
        normed_ref[pl.ds(pair * 256, 256), :] = normed
        both = lax.dot_general(
            weights, normed, (((1,), (1,)), ((), ())), preferred_element_type=jnp.float32
        )
        left = jax.nn.sigmoid(both[:CH]) * both[CH : 2 * CH]
        right = jax.nn.sigmoid(both[2 * CH : 3 * CH]) * both[3 * CH :]
        for member in range(2):
            slab = 2 * pair + member
            lanes = slice(member * 128, member * 128 + 128)
            wide[pl.ds(slab, CH, stride=PITCH), :] = left[:, lanes]
            wide[pl.ds(SLABS + slab, CH, stride=PITCH), :] = right[:, lanes]
    for c in range(CH):
        out_ref[pl.ds(c * 2 * SLABS, 2 * SLABS), :] = wide[pl.ds(c * PITCH, 2 * SLABS), :].astype(jnp.bfloat16)


def side_by_side(first, second, half):
    lanes = slice(half * 64, half * 64 + 64)
    return jnp.concatenate([first[:, lanes], second[:, lanes]], 1)


def mix_kernel(
    n_row, n_col, in_ref, gain_hbm, bias_hbm, out_ref, gain_ref, bias_ref, left, right, sems
):
    copies = [
        pltpu.make_async_copy(gain_hbm, gain_ref, sems.at[0]),
        pltpu.make_async_copy(bias_hbm, bias_ref, sems.at[1]),
    ]
    for copy in copies:
        copy.start()
    for r in range(n_row):
        for m in range(n_col // 2):
            start = (r * n_col + 2 * m) * 2 * SLABS
            first = in_ref[pl.ds(start, 2 * SLABS), :]
            second = in_ref[pl.ds(start + 2 * SLABS, 2 * SLABS), :]
            lanes = slice(m * 128, m * 128 + 128)
            for half in range(2):
                tile = side_by_side(first, second, half)
                rows = pl.ds(r * ROWS + half * HALF, HALF)
                left[rows, lanes] = tile[:SLABS]
                right[rows, lanes] = tile[SLABS:]
    for r in range(0, n_row, 8):
        block = lax.dot_general(
            left[pl.ds(r * ROWS, 8 * ROWS), :],
            right[...],
            (((1,), (1,)), ((), ())),
            preferred_element_type=jnp.float32,
        )
        for inner in range(8):
            for m in range(n_col // 2):
                lanes = slice(m * 128, m * 128 + 128)
                top = block[inner * ROWS : inner * ROWS + HALF, lanes]
                bottom = block[inner * ROWS + HALF : (inner + 1) * ROWS, lanes]
                for half in range(2):
                    start = ((r + inner) * n_col + 2 * m + half) * SLABS
                    out_ref[pl.ds(start, SLABS), :] = side_by_side(top, bottom, half).astype(
                        jnp.bfloat16
                    )
    for copy in copies:
        copy.wait()


def finish_kernel(mixed_ref, normed_ref, gain_ref, bias_ref, wg_ref, w_ref, out_hbm, wide, out_ref, sem):
    for c in range(CH):
        wide[pl.ds(c * OUT_PITCH, SLABS), :] = mixed_ref[pl.ds(c * SLABS, SLABS), :].astype(
            jnp.float32
        )
    total = jnp.zeros((SLABS, 128), jnp.float32)
    for c in range(CH):
        total += wide[pl.ds(c * OUT_PITCH, SLABS), :]
    mean = total / CH
    square = jnp.zeros((SLABS, 128), jnp.float32)
    for c in range(CH):
        square += jnp.square(wide[pl.ds(c * OUT_PITCH, SLABS), :] - mean)
    scale = lax.rsqrt(square / CH + EPS)
    gain = jnp.transpose(jnp.broadcast_to(gain_ref[...], (128, CH)))
    bias = jnp.transpose(jnp.broadcast_to(bias_ref[...], (128, CH)))
    gate_weights, weights = wg_ref[...], w_ref[...]
    for slab in range(SLABS):
        values = wide[pl.ds(slab, CH, stride=OUT_PITCH), :]
        normed = (values - mean[slab : slab + 1]) * scale[slab : slab + 1] * gain + bias
        projected = lax.dot_general(
            normed.astype(jnp.bfloat16),
            weights,
            (((0,), (0,)), ((), ())),
            preferred_element_type=jnp.float32,
        )
        gate = jnp.dot(
            normed_ref[pl.ds(slab * 128, 128), :], gate_weights, preferred_element_type=jnp.float32
        )
        update = jax.nn.sigmoid(gate) * projected
        low, high = pair_positions(slab)
        out_ref[pl.ds(low, COLS), :] = update[:COLS]
        out_ref[pl.ds(high, COLS), :] = update[COLS:]
    copy = pltpu.make_async_copy(out_ref, out_hbm, sem)
    copy.start()
    copy.wait()


def per_device(
    pair_rep,
    in_gain,
    in_bias,
    w_left_gate,
    w_left,
    w_right_gate,
    w_right,
    out_gain,
    out_bias,
    w_out_gate,
    w_out,
):
    n_row, n_col = lax.axis_size("row"), lax.axis_size("col")
    devices = n_row * n_col
    params = pltpu.CompilerParams(vmem_limit_bytes=48 << 20)
    flat = pair_rep.reshape(POSITIONS, CH)
    in_gain, in_bias = in_gain.reshape(1, CH), in_bias.reshape(1, CH)
    sent, normed = pl.pallas_call(
        project_kernel,
        out_shape=(
            jax.ShapeDtypeStruct((CH * 2 * SLABS, 128), jnp.bfloat16),
            jax.ShapeDtypeStruct((POSITIONS, CH), jnp.bfloat16),
        ),
        in_specs=[pl.BlockSpec(memory_space=pltpu.HBM)] * 7,
        scratch_shapes=[
            pltpu.VMEM((POSITIONS, CH), jnp.bfloat16),
            pltpu.VMEM((2, CH), jnp.float32),
            pltpu.VMEM((4, CH, CH), jnp.bfloat16),
            pltpu.VMEM((CH * PITCH, 128), jnp.float32),
            pltpu.SemaphoreType.DMA((7,)),
        ],
        compiler_params=params,
        name="project",
    )(*map(in_hbm, (flat, in_gain, in_bias, w_left_gate, w_left, w_right_gate, w_right)))
    arrived = lax.all_to_all(
        sent.reshape(devices, 2 * SLABS, 128), ("row", "col"), 0, 0, tiled=True
    )
    n_res = n_row * ROWS
    mixed, out_gain, out_bias = pl.pallas_call(
        lambda *refs: mix_kernel(n_row, n_col, *refs),
        out_shape=(
            jax.ShapeDtypeStruct((devices * SLABS, 128), jnp.bfloat16),
            jax.ShapeDtypeStruct((1, CH), jnp.float32),
            jax.ShapeDtypeStruct((1, CH), jnp.float32),
        ),
        in_specs=[pl.BlockSpec(memory_space=space) for space in (pltpu.VMEM, pltpu.HBM, pltpu.HBM)],
        scratch_shapes=[
            pltpu.VMEM((n_res, n_res), jnp.bfloat16),
            pltpu.VMEM((n_res, n_res), jnp.bfloat16),
            pltpu.SemaphoreType.DMA((2,)),
        ],
        compiler_params=params,
        name="mix",
    )(
        arrived.reshape(devices * 2 * SLABS, 128),
        in_hbm(out_gain.reshape(1, CH)),
        in_hbm(out_bias.reshape(1, CH)),
    )
    returned = lax.all_to_all(
        mixed.reshape(devices, SLABS, 128), ("row", "col"), 0, 0, tiled=True
    )
    update = pl.pallas_call(
        finish_kernel,
        out_shape=jax.ShapeDtypeStruct((POSITIONS, CH), jnp.float32),
        out_specs=pl.BlockSpec(memory_space=pltpu.HBM),
        scratch_shapes=[
            pltpu.VMEM((CH * OUT_PITCH, 128), jnp.float32),
            pltpu.VMEM((POSITIONS, CH), jnp.float32),
            pltpu.SemaphoreType.DMA,
        ],
        compiler_params=params,
        name="finish",
    )(
        returned.reshape(CH * SLABS, 128),
        normed,
        out_gain,
        out_bias,
        w_out_gate,
        w_out,
    )
    return update.reshape(ROWS, COLS, CH)


def solution(mesh):
    placed = (P("row", "col", None), P(), P(), P(), P(), P(), P(), P(), P(), P(), P())
    return jax.shard_map(
        per_device, mesh=mesh, in_specs=placed, out_specs=P("row", "col", None), check_vma=False
    )
```

```python
import jax
import jax.numpy as jnp
from jax import lax
from jax.experimental import pallas as pl
from jax.experimental.pallas import tpu as pltpu
from jax.sharding import PartitionSpec as P

EPS = 1e-05
CH = 128
ROWS, COLS = 32, 64
SLABS = ROWS * COLS // 128
HALF = ROWS // 2
POSITIONS = ROWS * COLS
PITCH = 36
OUT_PITCH = 20


def in_hbm(array):
    return pltpu.with_memory_space_constraint(array, pltpu.HBM)


def pair_positions(slab):
    return slab * COLS, HALF * COLS + slab * COLS


def input_norm(x_ref, gain, bias, slab):
    low, high = pair_positions(slab)
    values = jnp.concatenate([x_ref[pl.ds(low, COLS), :], x_ref[pl.ds(high, COLS), :]], 0)
    values = values.astype(jnp.float32)
    centred = values - jnp.mean(values, -1, keepdims=True)
    variance = jnp.mean(jnp.square(centred), -1, keepdims=True)
    return (centred * lax.rsqrt(variance + EPS) * gain + bias).astype(jnp.bfloat16)


def project_kernel(
    x_hbm, gain_hbm, bias_hbm, wlg_hbm, wl_hbm, wrg_hbm, wr_hbm, out_ref, normed_ref, x, norm, kept, wide, sems
):
    copies = [
        pltpu.make_async_copy(gain_hbm, norm.at[pl.ds(0, 1)], sems.at[0]),
        pltpu.make_async_copy(bias_hbm, norm.at[pl.ds(1, 1)], sems.at[1]),
    ]
    for k, w_hbm in enumerate((wlg_hbm, wl_hbm, wrg_hbm, wr_hbm)):
        copies.append(pltpu.make_async_copy(w_hbm, kept.at[k], sems.at[2 + k]))
    copy_x = pltpu.make_async_copy(x_hbm, x, sems.at[6])
    for copy in [copy_x] + copies:
        copy.start()
    for copy in copies:
        copy.wait()
    weights = jnp.concatenate([jnp.transpose(kept[k]) for k in range(4)], 0)
    gain, bias = norm[0:1, :], norm[1:2, :]
    copy_x.wait()
    for pair in range(SLABS // 2):
        normed = jnp.concatenate(
            [input_norm(x, gain, bias, 2 * pair + member) for member in range(2)], 0
        )
        normed_ref[pl.ds(pair * 256, 256), :] = normed
        both = lax.dot_general(
            weights, normed, (((1,), (1,)), ((), ())), preferred_element_type=jnp.float32
        )
        left = jax.nn.sigmoid(both[:CH]) * both[CH : 2 * CH]
        right = jax.nn.sigmoid(both[2 * CH : 3 * CH]) * both[3 * CH :]
        for member in range(2):
            slab = 2 * pair + member
            lanes = slice(member * 128, member * 128 + 128)
            wide[pl.ds(slab, CH, stride=PITCH), :] = left[:, lanes]
            wide[pl.ds(SLABS + slab, CH, stride=PITCH), :] = right[:, lanes]
    for c in range(CH):
        out_ref[pl.ds(c * 2 * SLABS, 2 * SLABS), :] = wide[pl.ds(c * PITCH, 2 * SLABS), :].astype(jnp.bfloat16)


def side_by_side(first, second, half):
    lanes = slice(half * 64, half * 64 + 64)
    return jnp.concatenate([first[:, lanes], second[:, lanes]], 1)


def mix_kernel(
    n_row, n_col, in_ref, gain_hbm, bias_hbm, out_ref, gain_ref, bias_ref, left, right, sems
):
    copies = [
        pltpu.make_async_copy(gain_hbm, gain_ref, sems.at[0]),
        pltpu.make_async_copy(bias_hbm, bias_ref, sems.at[1]),
    ]
    for copy in copies:
        copy.start()
    for r in range(n_row):
        for m in range(n_col // 2):
            start = (r * n_col + 2 * m) * 2 * SLABS
            first = in_ref[pl.ds(start, 2 * SLABS), :]
            second = in_ref[pl.ds(start + 2 * SLABS, 2 * SLABS), :]
            lanes = slice(m * 128, m * 128 + 128)
            for half in range(2):
                tile = side_by_side(first, second, half)
                rows = pl.ds(r * ROWS + half * HALF, HALF)
                left[rows, lanes] = tile[:SLABS]
                right[rows, lanes] = tile[SLABS:]
    for r in range(0, n_row, 8):
        block = lax.dot_general(
            left[pl.ds(r * ROWS, 8 * ROWS), :],
            right[...],
            (((1,), (1,)), ((), ())),
            preferred_element_type=jnp.float32,
        )
        for inner in range(8):
            for m in range(n_col // 2):
                lanes = slice(m * 128, m * 128 + 128)
                top = block[inner * ROWS : inner * ROWS + HALF, lanes]
                bottom = block[inner * ROWS + HALF : (inner + 1) * ROWS, lanes]
                for half in range(2):
                    start = ((r + inner) * n_col + 2 * m + half) * SLABS
                    out_ref[pl.ds(start, SLABS), :] = side_by_side(top, bottom, half).astype(
                        jnp.bfloat16
                    )
    for copy in copies:
        copy.wait()


def finish_kernel(mixed_ref, normed_ref, gain_ref, bias_ref, wg_ref, w_ref, out_hbm, wide, out_ref, sem):
    total = [jnp.zeros((SLABS, 128), jnp.float32)] * 8
    for c in range(CH):
        values = mixed_ref[pl.ds(c * SLABS, SLABS), :].astype(jnp.float32)
        wide[pl.ds(c * OUT_PITCH, SLABS), :] = values
        total[c % 8] += values
    mean = sum(total[1:], total[0]) / CH
    square = [jnp.zeros((SLABS, 128), jnp.float32)] * 8
    for c in range(CH):
        values = mixed_ref[pl.ds(c * SLABS, SLABS), :].astype(jnp.float32)
        square[c % 8] += jnp.square(values - mean)
    scale = lax.rsqrt(sum(square[1:], square[0]) / CH + EPS)
    gain = jnp.transpose(jnp.broadcast_to(gain_ref[...], (128, CH)))
    bias = jnp.transpose(jnp.broadcast_to(bias_ref[...], (128, CH)))
    gate_weights, weights = wg_ref[...], w_ref[...]
    copies = []
    for first in range(0, SLABS, 4):
        columns = []
        for slab in range(first, first + 4):
            values = wide[pl.ds(slab, CH, stride=OUT_PITCH), :]
            normed = (values - mean[slab : slab + 1]) * scale[slab : slab + 1] * gain + bias
            columns.append(normed.astype(jnp.bfloat16))
        projected = lax.dot_general(
            jnp.concatenate(columns, 1),
            weights,
            (((0,), (0,)), ((), ())),
            preferred_element_type=jnp.float32,
        )
        gate = jnp.dot(
            normed_ref[pl.ds(first * 128, 4 * 128), :],
            gate_weights,
            preferred_element_type=jnp.float32,
        )
        update = jax.nn.sigmoid(gate) * projected
        for member in range(4):
            low, high = pair_positions(first + member)
            middle = member * 128 + COLS
            out_ref[pl.ds(low, COLS), :] = update[middle - COLS : middle]
            out_ref[pl.ds(high, COLS), :] = update[middle : middle + COLS]
        if first + 4 in (8, SLABS):
            begin = 0 if first + 4 == 8 else 8
            for start in pair_positions(begin):
                rows = pl.ds(start, (first + 4 - begin) * COLS)
                copies.append(
                    pltpu.make_async_copy(out_ref.at[rows], out_hbm.at[rows], sem.at[len(copies)])
                )
                copies[-1].start()
    for copy in copies:
        copy.wait()


def per_device(
    pair_rep,
    in_gain,
    in_bias,
    w_left_gate,
    w_left,
    w_right_gate,
    w_right,
    out_gain,
    out_bias,
    w_out_gate,
    w_out,
):
    n_row, n_col = lax.axis_size("row"), lax.axis_size("col")
    devices = n_row * n_col
    params = pltpu.CompilerParams(vmem_limit_bytes=48 << 20)
    flat = pair_rep.reshape(POSITIONS, CH)
    in_gain, in_bias = in_gain.reshape(1, CH), in_bias.reshape(1, CH)
    sent, normed = pl.pallas_call(
        project_kernel,
        out_shape=(
            jax.ShapeDtypeStruct((CH * 2 * SLABS, 128), jnp.bfloat16),
            jax.ShapeDtypeStruct((POSITIONS, CH), jnp.bfloat16),
        ),
        in_specs=[pl.BlockSpec(memory_space=pltpu.HBM)] * 7,
        scratch_shapes=[
            pltpu.VMEM((POSITIONS, CH), jnp.bfloat16),
            pltpu.VMEM((2, CH), jnp.float32),
            pltpu.VMEM((4, CH, CH), jnp.bfloat16),
            pltpu.VMEM(((CH + 2) * PITCH, 128), jnp.float32),
            pltpu.SemaphoreType.DMA((7,)),
        ],
        compiler_params=params,
        name="project",
    )(*map(in_hbm, (flat, in_gain, in_bias, w_left_gate, w_left, w_right_gate, w_right)))
    arrived = lax.all_to_all(
        sent.reshape(devices, 2 * SLABS, 128), ("row", "col"), 0, 0, tiled=True
    )
    n_res = n_row * ROWS
    mixed, out_gain, out_bias = pl.pallas_call(
        lambda *refs: mix_kernel(n_row, n_col, *refs),
        out_shape=(
            jax.ShapeDtypeStruct((devices * SLABS, 128), jnp.bfloat16),
            jax.ShapeDtypeStruct((1, CH), jnp.float32),
            jax.ShapeDtypeStruct((1, CH), jnp.float32),
        ),
        in_specs=[pl.BlockSpec(memory_space=space) for space in (pltpu.VMEM, pltpu.HBM, pltpu.HBM)],
        scratch_shapes=[
            pltpu.VMEM((n_res, n_res), jnp.bfloat16),
            pltpu.VMEM((n_res, n_res), jnp.bfloat16),
            pltpu.SemaphoreType.DMA((2,)),
        ],
        compiler_params=params,
        name="mix",
    )(
        arrived.reshape(devices * 2 * SLABS, 128),
        in_hbm(out_gain.reshape(1, CH)),
        in_hbm(out_bias.reshape(1, CH)),
    )
    returned = lax.all_to_all(
        mixed.reshape(devices, SLABS, 128), ("row", "col"), 0, 0, tiled=True
    )
    update = pl.pallas_call(
        finish_kernel,
        out_shape=jax.ShapeDtypeStruct((POSITIONS, CH), jnp.float32),
        out_specs=pl.BlockSpec(memory_space=pltpu.HBM),
        scratch_shapes=[
            pltpu.VMEM(((CH + 2) * OUT_PITCH, 128), jnp.float32),
            pltpu.VMEM((POSITIONS, CH), jnp.float32),
            pltpu.SemaphoreType.DMA((4,)),
        ],
        compiler_params=params,
        name="finish",
    )(
        returned.reshape(CH * SLABS, 128),
        normed,
        out_gain,
        out_bias,
        w_out_gate,
        w_out,
    )
    return update.reshape(ROWS, COLS, CH)


def solution(mesh):
    placed = (P("row", "col", None), P(), P(), P(), P(), P(), P(), P(), P(), P(), P())
    return jax.shard_map(
        per_device, mesh=mesh, in_specs=placed, out_specs=P("row", "col", None), check_vma=False
    )
```

```python
import jax
import jax.numpy as jnp
from jax import lax
from jax.experimental import pallas as pl
from jax.experimental.pallas import tpu as pltpu
from jax.sharding import PartitionSpec as P

EPS = 1e-05
CH = 128
ROWS, COLS = 32, 64
SLABS = ROWS * COLS // 128
HALF = ROWS // 2
POSITIONS = ROWS * COLS
PITCH = 36
OUT_PITCH = 20


def in_hbm(array):
    return pltpu.with_memory_space_constraint(array, pltpu.HBM)


def pair_positions(slab):
    return slab * COLS, HALF * COLS + slab * COLS


def input_norm(x_ref, gain, bias, slab):
    low, high = pair_positions(slab)
    values = jnp.concatenate([x_ref[pl.ds(low, COLS), :], x_ref[pl.ds(high, COLS), :]], 0)
    values = values.astype(jnp.float32)
    centred = values - jnp.mean(values, -1, keepdims=True)
    variance = jnp.mean(jnp.square(centred), -1, keepdims=True)
    return (centred * lax.rsqrt(variance + EPS) * gain + bias).astype(jnp.bfloat16)


def project_kernel(
    x_hbm, gain_hbm, bias_hbm, wlg_hbm, wl_hbm, wrg_hbm, wr_hbm, out_ref, normed_ref, x, norm, kept, wide, sems
):
    copies = [
        pltpu.make_async_copy(gain_hbm, norm.at[pl.ds(0, 1)], sems.at[0]),
        pltpu.make_async_copy(bias_hbm, norm.at[pl.ds(1, 1)], sems.at[1]),
    ]
    for k, w_hbm in enumerate((wlg_hbm, wl_hbm, wrg_hbm, wr_hbm)):
        copies.append(pltpu.make_async_copy(w_hbm, kept.at[k], sems.at[2 + k]))
    copy_x = pltpu.make_async_copy(x_hbm, x, sems.at[6])
    for copy in [copy_x] + copies:
        copy.start()
    for copy in copies:
        copy.wait()
    weights = jnp.concatenate([jnp.transpose(kept[k]) for k in range(4)], 0)
    gain, bias = norm[0:1, :], norm[1:2, :]
    copy_x.wait()
    for pair in range(SLABS // 2):
        normed = jnp.concatenate(
            [input_norm(x, gain, bias, 2 * pair + member) for member in range(2)], 0
        )
        normed_ref[pl.ds(pair * 256, 256), :] = normed
        both = lax.dot_general(
            weights, normed, (((1,), (1,)), ((), ())), preferred_element_type=jnp.float32
        )
        left = jax.nn.sigmoid(both[:CH]) * both[CH : 2 * CH]
        right = jax.nn.sigmoid(both[2 * CH : 3 * CH]) * both[3 * CH :]
        for member in range(2):
            slab = 2 * pair + member
            lanes = slice(member * 128, member * 128 + 128)
            wide[pl.ds(slab, CH, stride=PITCH), :] = left[:, lanes]
            wide[pl.ds(SLABS + slab, CH, stride=PITCH), :] = right[:, lanes]
    for c in range(CH):
        out_ref[pl.ds(c * 2 * SLABS, 2 * SLABS), :] = wide[pl.ds(c * PITCH, 2 * SLABS), :].astype(jnp.bfloat16)


def side_by_side(first, second, half):
    lanes = slice(half * 64, half * 64 + 64)
    return jnp.concatenate([first[:, lanes], second[:, lanes]], 1)


def mix_kernel(
    n_row, n_col, in_ref, gain_hbm, bias_hbm, out_ref, gain_ref, bias_ref, left, right, sems
):
    copies = [
        pltpu.make_async_copy(gain_hbm, gain_ref, sems.at[0]),
        pltpu.make_async_copy(bias_hbm, bias_ref, sems.at[1]),
    ]
    for copy in copies:
        copy.start()
    for r in range(n_row):
        for m in range(n_col // 2):
            start = (r * n_col + 2 * m) * 2 * SLABS
            first = in_ref[pl.ds(start, 2 * SLABS), :]
            second = in_ref[pl.ds(start + 2 * SLABS, 2 * SLABS), :]
            lanes = slice(m * 128, m * 128 + 128)
            for half in range(2):
                tile = side_by_side(first, second, half)
                rows = pl.ds(r * ROWS + half * HALF, HALF)
                left[rows, lanes] = tile[:SLABS]
                right[rows, lanes] = tile[SLABS:]
    for r in range(0, n_row, 8):
        block = lax.dot_general(
            left[pl.ds(r * ROWS, 8 * ROWS), :],
            right[...],
            (((1,), (1,)), ((), ())),
            preferred_element_type=jnp.float32,
        )
        for inner in range(8):
            for m in range(n_col // 2):
                lanes = slice(m * 128, m * 128 + 128)
                top = block[inner * ROWS : inner * ROWS + HALF, lanes]
                bottom = block[inner * ROWS + HALF : (inner + 1) * ROWS, lanes]
                for half in range(2):
                    start = ((r + inner) * n_col + 2 * m + half) * SLABS
                    out_ref[pl.ds(start, SLABS), :] = side_by_side(top, bottom, half).astype(
                        jnp.bfloat16
                    )
    for copy in copies:
        copy.wait()


def finish_kernel(mixed_ref, normed_ref, gain_ref, bias_ref, wg_ref, w_ref, out_hbm, wide, out_ref, sem):
    total = [jnp.zeros((SLABS, 128), jnp.float32)] * 8
    for c in range(CH):
        values = mixed_ref[pl.ds(c * SLABS, SLABS), :].astype(jnp.float32)
        wide[pl.ds(c * OUT_PITCH, SLABS), :] = values
        total[c % 8] += values
    mean = sum(total[1:], total[0]) / CH
    square = [jnp.zeros((SLABS, 128), jnp.float32)] * 8
    for c in range(CH):
        values = mixed_ref[pl.ds(c * SLABS, SLABS), :].astype(jnp.float32)
        square[c % 8] += jnp.square(values - mean)
    scale = lax.rsqrt(sum(square[1:], square[0]) / CH + EPS)
    gain = jnp.transpose(jnp.broadcast_to(gain_ref[...], (128, CH)))
    bias = jnp.transpose(jnp.broadcast_to(bias_ref[...], (128, CH)))
    gate_weights, weights = wg_ref[...], w_ref[...]
    copies = []
    for first in range(0, SLABS, 4):
        columns = []
        for slab in range(first, first + 4):
            values = wide[pl.ds(slab, CH, stride=OUT_PITCH), :]
            normed = (values - mean[slab : slab + 1]) * scale[slab : slab + 1] * gain + bias
            columns.append(normed.astype(jnp.bfloat16))
        projected = lax.dot_general(
            jnp.concatenate(columns, 1),
            weights,
            (((0,), (0,)), ((), ())),
            preferred_element_type=jnp.float32,
        )
        gate = jnp.dot(
            normed_ref[pl.ds(first * 128, 4 * 128), :],
            gate_weights,
            preferred_element_type=jnp.float32,
        )
        update = jax.nn.sigmoid(gate) * projected
        for member in range(4):
            rows = pl.ds((first + member) * COLS, COLS)
            middle = member * 128 + COLS
            out_ref[0, rows, :] = update[middle - COLS : middle]
            out_ref[1, rows, :] = update[middle : middle + COLS]
        if first + 4 in (4, 8, 12, 16):
            begin = first + 4 - 4
            rows = pl.ds(begin * COLS, 4 * COLS)
            copies.append(
                pltpu.make_async_copy(out_ref.at[:, rows], out_hbm.at[:, rows], sem.at[len(copies)])
            )
            copies[-1].start()
    for copy in copies:
        copy.wait()


def per_device(
    pair_rep,
    in_gain,
    in_bias,
    w_left_gate,
    w_left,
    w_right_gate,
    w_right,
    out_gain,
    out_bias,
    w_out_gate,
    w_out,
):
    n_row, n_col = lax.axis_size("row"), lax.axis_size("col")
    devices = n_row * n_col
    params = pltpu.CompilerParams(vmem_limit_bytes=48 << 20)
    flat = pair_rep.reshape(POSITIONS, CH)
    in_gain, in_bias = in_gain.reshape(1, CH), in_bias.reshape(1, CH)
    sent, normed = pl.pallas_call(
        project_kernel,
        out_shape=(
            jax.ShapeDtypeStruct((CH * 2 * SLABS, 128), jnp.bfloat16),
            jax.ShapeDtypeStruct((POSITIONS, CH), jnp.bfloat16),
        ),
        in_specs=[pl.BlockSpec(memory_space=pltpu.HBM)] * 7,
        scratch_shapes=[
            pltpu.VMEM((POSITIONS, CH), jnp.bfloat16),
            pltpu.VMEM((2, CH), jnp.float32),
            pltpu.VMEM((4, CH, CH), jnp.bfloat16),
            pltpu.VMEM(((CH + 2) * PITCH, 128), jnp.float32),
            pltpu.SemaphoreType.DMA((7,)),
        ],
        compiler_params=params,
        name="project",
    )(*map(in_hbm, (flat, in_gain, in_bias, w_left_gate, w_left, w_right_gate, w_right)))
    arrived = lax.all_to_all(
        sent.reshape(devices, 2 * SLABS, 128), ("row", "col"), 0, 0, tiled=True
    )
    n_res = n_row * ROWS
    mixed, out_gain, out_bias = pl.pallas_call(
        lambda *refs: mix_kernel(n_row, n_col, *refs),
        out_shape=(
            jax.ShapeDtypeStruct((devices * SLABS, 128), jnp.bfloat16),
            jax.ShapeDtypeStruct((1, CH), jnp.float32),
            jax.ShapeDtypeStruct((1, CH), jnp.float32),
        ),
        in_specs=[pl.BlockSpec(memory_space=space) for space in (pltpu.VMEM, pltpu.HBM, pltpu.HBM)],
        scratch_shapes=[
            pltpu.VMEM((n_res, n_res), jnp.bfloat16),
            pltpu.VMEM((n_res, n_res), jnp.bfloat16),
            pltpu.SemaphoreType.DMA((2,)),
        ],
        compiler_params=params,
        name="mix",
    )(
        arrived.reshape(devices * 2 * SLABS, 128),
        in_hbm(out_gain.reshape(1, CH)),
        in_hbm(out_bias.reshape(1, CH)),
    )
    returned = lax.all_to_all(
        mixed.reshape(devices, SLABS, 128), ("row", "col"), 0, 0, tiled=True
    )
    update = pl.pallas_call(
        finish_kernel,
        out_shape=jax.ShapeDtypeStruct((2, POSITIONS // 2, CH), jnp.float32),
        out_specs=pl.BlockSpec(memory_space=pltpu.HBM),
        scratch_shapes=[
            pltpu.VMEM(((CH + 2) * OUT_PITCH, 128), jnp.float32),
            pltpu.VMEM((2, POSITIONS // 2, CH), jnp.float32),
            pltpu.SemaphoreType.DMA((4,)),
        ],
        compiler_params=params,
        name="finish",
    )(
        returned.reshape(CH * SLABS, 128),
        normed,
        out_gain,
        out_bias,
        w_out_gate,
        w_out,
    )
    return update.reshape(ROWS, COLS, CH)


def solution(mesh):
    placed = (P("row", "col", None), P(), P(), P(), P(), P(), P(), P(), P(), P(), P())
    return jax.shard_map(
        per_device, mesh=mesh, in_specs=placed, out_specs=P("row", "col", None), check_vma=False
    )
```

```python
import jax
import jax.numpy as jnp
from jax import lax
from jax.experimental import pallas as pl
from jax.experimental.pallas import tpu as pltpu
from jax.sharding import PartitionSpec as P

EPS = 1e-05
CH = 128
ROWS, COLS = 32, 64
SLABS = ROWS * COLS // 128
HALF = ROWS // 2
POSITIONS = ROWS * COLS
PITCH = 36
OUT_PITCH = 20


def in_hbm(array):
    return pltpu.with_memory_space_constraint(array, pltpu.HBM)


def pair_positions(slab):
    return slab * COLS, HALF * COLS + slab * COLS


def input_norm(x_ref, gain, bias, slab):
    low, high = pair_positions(slab)
    values = jnp.concatenate([x_ref[pl.ds(low, COLS), :], x_ref[pl.ds(high, COLS), :]], 0)
    values = values.astype(jnp.float32)
    centred = values - jnp.mean(values, -1, keepdims=True)
    variance = jnp.mean(jnp.square(centred), -1, keepdims=True)
    return (centred * lax.rsqrt(variance + EPS) * gain + bias).astype(jnp.bfloat16)


def project_kernel(
    x_hbm, gain_hbm, bias_hbm, wlg_hbm, wl_hbm, wrg_hbm, wr_hbm, out_ref, normed_ref, x, norm, kept, wide, sems
):
    copies = [
        pltpu.make_async_copy(gain_hbm, norm.at[pl.ds(0, 1)], sems.at[0]),
        pltpu.make_async_copy(bias_hbm, norm.at[pl.ds(1, 1)], sems.at[1]),
    ]
    for k, w_hbm in enumerate((wlg_hbm, wl_hbm, wrg_hbm, wr_hbm)):
        copies.append(pltpu.make_async_copy(w_hbm, kept.at[k], sems.at[2 + k]))
    copy_x = pltpu.make_async_copy(x_hbm, x, sems.at[6])
    for copy in [copy_x] + copies:
        copy.start()
    for copy in copies:
        copy.wait()
    weights = jnp.concatenate([jnp.transpose(kept[k]) for k in range(4)], 0)
    gain, bias = norm[0:1, :], norm[1:2, :]
    copy_x.wait()
    for pair in range(SLABS // 4):
        normed = jnp.concatenate(
            [input_norm(x, gain, bias, 4 * pair + member) for member in range(4)], 0
        )
        normed_ref[pl.ds(pair * 512, 512), :] = normed
        both = lax.dot_general(
            weights, normed, (((1,), (1,)), ((), ())), preferred_element_type=jnp.float32
        )
        left = jax.nn.sigmoid(both[:CH]) * both[CH : 2 * CH]
        right = jax.nn.sigmoid(both[2 * CH : 3 * CH]) * both[3 * CH :]
        for member in range(4):
            slab = 4 * pair + member
            lanes = slice(member * 128, member * 128 + 128)
            wide[pl.ds(slab, CH, stride=PITCH), :] = left[:, lanes]
            wide[pl.ds(SLABS + slab, CH, stride=PITCH), :] = right[:, lanes]
    for c in range(CH):
        out_ref[pl.ds(c * 2 * SLABS, 2 * SLABS), :] = wide[pl.ds(c * PITCH, 2 * SLABS), :].astype(jnp.bfloat16)


def side_by_side(first, second, half):
    lanes = slice(half * 64, half * 64 + 64)
    return jnp.concatenate([first[:, lanes], second[:, lanes]], 1)


def mix_kernel(
    n_row, n_col, in_ref, gain_hbm, bias_hbm, out_ref, gain_ref, bias_ref, left, right, sems
):
    copies = [
        pltpu.make_async_copy(gain_hbm, gain_ref, sems.at[0]),
        pltpu.make_async_copy(bias_hbm, bias_ref, sems.at[1]),
    ]
    for copy in copies:
        copy.start()
    for r in range(n_row):
        for m in range(n_col // 2):
            start = (r * n_col + 2 * m) * 2 * SLABS
            first = in_ref[pl.ds(start, 2 * SLABS), :]
            second = in_ref[pl.ds(start + 2 * SLABS, 2 * SLABS), :]
            lanes = slice(m * 128, m * 128 + 128)
            for half in range(2):
                tile = side_by_side(first, second, half)
                rows = pl.ds(r * ROWS + half * HALF, HALF)
                left[rows, lanes] = tile[:SLABS]
                right[rows, lanes] = tile[SLABS:]
    for r in range(0, n_row, 8):
        block = lax.dot_general(
            left[pl.ds(r * ROWS, 8 * ROWS), :],
            right[...],
            (((1,), (1,)), ((), ())),
            preferred_element_type=jnp.float32,
        ).astype(jnp.bfloat16)
        for inner in range(8):
            for m in range(n_col // 2):
                lanes = slice(m * 128, m * 128 + 128)
                top = block[inner * ROWS : inner * ROWS + HALF, lanes]
                bottom = block[inner * ROWS + HALF : (inner + 1) * ROWS, lanes]
                for half in range(2):
                    start = ((r + inner) * n_col + 2 * m + half) * SLABS
                    out_ref[pl.ds(start, SLABS), :] = side_by_side(top, bottom, half)
    for copy in copies:
        copy.wait()


def finish_kernel(mixed_ref, normed_ref, gain_ref, bias_ref, wg_ref, w_ref, out_hbm, wide, out_ref, sem):
    total = [jnp.zeros((SLABS, 128), jnp.float32)] * 8
    for c in range(CH):
        values = mixed_ref[pl.ds(c * SLABS, SLABS), :].astype(jnp.float32)
        wide[pl.ds(c * OUT_PITCH, SLABS), :] = values
        total[c % 8] += values
    mean = sum(total[1:], total[0]) / CH
    square = [jnp.zeros((SLABS, 128), jnp.float32)] * 8
    for c in range(CH):
        values = mixed_ref[pl.ds(c * SLABS, SLABS), :].astype(jnp.float32)
        square[c % 8] += jnp.square(values - mean)
    scale = lax.rsqrt(sum(square[1:], square[0]) / CH + EPS)
    gain = jnp.transpose(jnp.broadcast_to(gain_ref[...], (128, CH)))
    bias = jnp.transpose(jnp.broadcast_to(bias_ref[...], (128, CH)))
    gate_weights, weights = wg_ref[...], w_ref[...]
    copies = []
    for first in range(0, SLABS, 4):
        columns = []
        for slab in range(first, first + 4):
            values = wide[pl.ds(slab, CH, stride=OUT_PITCH), :]
            normed = (values - mean[slab : slab + 1]) * scale[slab : slab + 1] * gain + bias
            columns.append(normed.astype(jnp.bfloat16))
        projected = lax.dot_general(
            jnp.concatenate(columns, 1),
            weights,
            (((0,), (0,)), ((), ())),
            preferred_element_type=jnp.float32,
        )
        gate = jnp.dot(
            normed_ref[pl.ds(first * 128, 4 * 128), :],
            gate_weights,
            preferred_element_type=jnp.float32,
        )
        update = jax.nn.sigmoid(gate) * projected
        for member in range(4):
            rows = pl.ds((first + member) * COLS, COLS)
            middle = member * 128 + COLS
            out_ref[0, rows, :] = update[middle - COLS : middle]
            out_ref[1, rows, :] = update[middle : middle + COLS]
        if first + 4 in (4, 8, 12, 16):
            begin = first + 4 - 4
            rows = pl.ds(begin * COLS, 4 * COLS)
            copies.append(
                pltpu.make_async_copy(out_ref.at[:, rows], out_hbm.at[:, rows], sem.at[len(copies)])
            )
            copies[-1].start()
    for copy in copies:
        copy.wait()


def per_device(
    pair_rep,
    in_gain,
    in_bias,
    w_left_gate,
    w_left,
    w_right_gate,
    w_right,
    out_gain,
    out_bias,
    w_out_gate,
    w_out,
):
    n_row, n_col = lax.axis_size("row"), lax.axis_size("col")
    devices = n_row * n_col
    params = pltpu.CompilerParams(vmem_limit_bytes=48 << 20)
    flat = pair_rep.reshape(POSITIONS, CH)
    in_gain, in_bias = in_gain.reshape(1, CH), in_bias.reshape(1, CH)
    sent, normed = pl.pallas_call(
        project_kernel,
        out_shape=(
            jax.ShapeDtypeStruct((CH * 2 * SLABS, 128), jnp.bfloat16),
            jax.ShapeDtypeStruct((POSITIONS, CH), jnp.bfloat16),
        ),
        in_specs=[pl.BlockSpec(memory_space=pltpu.HBM)] * 7,
        scratch_shapes=[
            pltpu.VMEM((POSITIONS, CH), jnp.bfloat16),
            pltpu.VMEM((2, CH), jnp.float32),
            pltpu.VMEM((4, CH, CH), jnp.bfloat16),
            pltpu.VMEM(((CH + 2) * PITCH, 128), jnp.float32),
            pltpu.SemaphoreType.DMA((7,)),
        ],
        compiler_params=params,
        name="project",
    )(*map(in_hbm, (flat, in_gain, in_bias, w_left_gate, w_left, w_right_gate, w_right)))
    arrived = lax.all_to_all(
        sent.reshape(devices, 2 * SLABS, 128), ("row", "col"), 0, 0, tiled=True
    )
    n_res = n_row * ROWS
    mixed, out_gain, out_bias = pl.pallas_call(
        lambda *refs: mix_kernel(n_row, n_col, *refs),
        out_shape=(
            jax.ShapeDtypeStruct((devices * SLABS, 128), jnp.bfloat16),
            jax.ShapeDtypeStruct((1, CH), jnp.float32),
            jax.ShapeDtypeStruct((1, CH), jnp.float32),
        ),
        in_specs=[pl.BlockSpec(memory_space=space) for space in (pltpu.VMEM, pltpu.HBM, pltpu.HBM)],
        scratch_shapes=[
            pltpu.VMEM((n_res, n_res), jnp.bfloat16),
            pltpu.VMEM((n_res, n_res), jnp.bfloat16),
            pltpu.SemaphoreType.DMA((2,)),
        ],
        compiler_params=params,
        name="mix",
    )(
        arrived.reshape(devices * 2 * SLABS, 128),
        in_hbm(out_gain.reshape(1, CH)),
        in_hbm(out_bias.reshape(1, CH)),
    )
    returned = lax.all_to_all(
        mixed.reshape(devices, SLABS, 128), ("row", "col"), 0, 0, tiled=True
    )
    update = pl.pallas_call(
        finish_kernel,
        out_shape=jax.ShapeDtypeStruct((2, POSITIONS // 2, CH), jnp.float32),
        out_specs=pl.BlockSpec(memory_space=pltpu.HBM),
        scratch_shapes=[
            pltpu.VMEM(((CH + 2) * OUT_PITCH, 128), jnp.float32),
            pltpu.VMEM((2, POSITIONS // 2, CH), jnp.float32),
            pltpu.SemaphoreType.DMA((4,)),
        ],
        compiler_params=params,
        name="finish",
    )(
        returned.reshape(CH * SLABS, 128),
        normed,
        out_gain,
        out_bias,
        w_out_gate,
        w_out,
    )
    return update.reshape(ROWS, COLS, CH)


def solution(mesh):
    placed = (P("row", "col", None), P(), P(), P(), P(), P(), P(), P(), P(), P(), P())
    return jax.shard_map(
        per_device, mesh=mesh, in_specs=placed, out_specs=P("row", "col", None), check_vma=False
    )
```
